512 devices in a mesh: grp: 16 (over x, y), dev: 32 (over z, core).
Axes of the slice: x: 4, y: 4, z: 16, core: 2. Of those that a mesh axis runs over, the one named last changes fastest.
Arguments:
- right_side: float32 [3584, 22, 896], P(('grp', 'dev')), may hold values from -9 to 9
- screening: float32 [3584, 22, 896], P(('grp', 'dev')), may hold values from 0.01 to 8
Outputs:
- solution_field: float32 [3584, 22, 896], P(('grp', 'dev'))
- residual: float32 [3584, 22, 896], P(('grp', 'dev'))
The draws below stay inside these ranges and needn't reach their ends.
All inputs are finite; a program needn't handle non-finite values.
Results may differ from the reference program's by a relative error of at most 0.0003.
Values sent between devices are 32-bit elements; how exact they have to be, the bound alone decides.
No kernel may reach another device: no remote copies, remote signals or barrier semaphores. Data moves between devices by JAX's collectives and lax.ppermute only.
A program may use at most 64 MiB of HBM per device.

```python
import math
import jax
import jax.numpy as jnp
import numpy as np
from jax import lax

EY = 3
EZ = 128
ITERS = 2
CSWEEPS = 3
NX = 3584
NY = 22
NZ = 896


def draw_right_side(key, part):
    growth = 1.0 + 2.0 * jnp.arange(NX, dtype=jnp.float32) / (NX - 1)
    normal_part = jax.random.truncated_normal(key, -3.0, 3.0, (NX, NY, NZ), jnp.float32)
    return normal_part * growth[:, None, None]


def draw_screening(key, part):
    position = jnp.arange(NX, dtype=jnp.float32) / (NX - 1)
    growth = jnp.exp(math.log(4.0) * position)[:, None, None]
    sample = jnp.exp(jax.random.uniform(key, (NX, NY, NZ), jnp.float32, math.log(0.01), math.log(2.0)))
    return sample * growth


def setup_inputs(seed: int = 0) -> dict:
    key_of = jax.random.split(jax.random.key(seed), 3)
    return {
        "right_side": draw_right_side(jax.random.fold_in(key_of[2], 71), 0),
        "screening": draw_screening(jax.random.fold_in(key_of[2], 71), 0),
    }


damping = 0.6


def legendre_seven(points):
    return (429.0 * points ** 7 - 693.0 * points ** 5 + 315.0 * points ** 3 - 35.0 * points) / 16.0


def pad_vector(vector, before, after):
    return np.concatenate([np.zeros(before), vector, np.zeros(after)])


def pad_matrix(matrix, before, after):
    width = matrix.shape[1]
    rows = np.concatenate([np.zeros((before, width)), matrix, np.zeros((after, width))], axis=0)
    height = rows.shape[0]
    return np.concatenate([np.zeros((height, before)), rows, np.zeros((height, after))], axis=1)


def diag_entries(matrix):
    return np.array([matrix[k, k] for k in range(matrix.shape[0])])


def diag_matrix(vector):
    count = vector.shape[0]
    return np.stack([pad_vector(np.array([vector[k]]), k, count - 1 - k) for k in range(count)])


def gll_tables():
    gll_nodes = np.array([-1.0, -0.8717401485096066, -0.5917001814331423, -0.2092992179024789,
                          0.2092992179024789, 0.5917001814331423, 0.8717401485096066, 1.0])
    values = legendre_seven(gll_nodes)
    weights = 2.0 / (56.0 * values * values)
    spacing = gll_nodes[:, None] - gll_nodes[None, :]
    distinct = np.abs(spacing) > 1e-12
    divisor = np.where(distinct, spacing, 1.0)
    derivative = np.where(distinct, (values[:, None] / values[None, :]) / divisor, 0.0)
    derivative = derivative + diag_matrix(np.array([-14.0, 0.0, 0.0, 0.0, 0.0, 0.0, 0.0, 14.0]))
    stiffness = derivative.T @ (weights[:, None] * derivative)
    return gll_nodes, weights, stiffness


def tables(elems_y):
    gll_nodes, weights, stiffness = gll_tables()
    count_y = 7 * elems_y + 1
    mass_y = np.zeros(count_y)
    stiff_y = np.zeros((count_y, count_y))
    coarse_stiff_y = np.zeros((elems_y + 1, elems_y + 1))
    pair_stiff = np.array([[0.5, -0.5], [-0.5, 0.5]])
    phi_low = (1.0 - gll_nodes) / 2.0
    phi_high = (1.0 + gll_nodes) / 2.0
    for element in range(elems_y):
        before = 7 * element
        trailing = count_y - 8 - before
        mass_y = mass_y + pad_vector(weights, before, trailing)
        stiff_y = stiff_y + pad_matrix(stiffness, before, trailing)
        coarse_stiff_y = coarse_stiff_y + pad_matrix(pair_stiff, element, elems_y - 1 - element)
    row_list = []
    for node_index in range(count_y):
        element = min(node_index // 7, elems_y - 1)
        offset = node_index - 7 * element
        row_list.append(pad_vector(np.array([phi_low[offset], phi_high[offset]]), element, elems_y - 1 - element))
    interp_y = np.stack(row_list)
    stiff_diag = diag_entries(stiffness)
    mass_edge = np.concatenate([np.array([weights[0] + weights[7]]), weights[1:7]])
    stiff_edge = np.concatenate([np.array([stiff_diag[0] + stiff_diag[7]]), stiff_diag[1:7]])
    coarse_mass_y = np.concatenate([np.array([1.0]), np.full(elems_y - 1, 2.0), np.array([1.0])])
    entry_list = [stiffness, mass_edge, stiff_edge, mass_y, stiff_y, diag_entries(stiff_y), interp_y,
                  phi_low[:7], phi_high[:7], coarse_stiff_y, coarse_mass_y, diag_entries(coarse_stiff_y)]
    return [jnp.asarray(entry_table, jnp.float32) for entry_table in entry_list]


def stiff_along_y(grid_values, stiff_y):
    return jnp.einsum("mn,xnz->xmz", stiff_y, grid_values, precision=lax.Precision.HIGHEST)


def stiff_along_z(grid_values, stiffness):
    planes, count_y, count_z = grid_values.shape
    blocks = grid_values.reshape(planes, count_y, 7, count_z // 7)
    extended = jnp.concatenate([blocks, jnp.roll(blocks[:, :, :1], -1, axis=3)], axis=2)
    product = jnp.einsum("ij,xyjz->xyiz", stiffness, extended, precision=lax.Precision.HIGHEST)
    folded = jnp.concatenate([product[:, :, :1] + jnp.roll(product[:, :, 7:8], 1, axis=3), product[:, :, 1:7]], axis=2)
    return folded.reshape(planes, count_y, count_z)


def stiff_along_x(grid_values, stiffness):
    planes, count_y, count_z = grid_values.shape
    blocks = grid_values.reshape(planes // 7, 7, count_y, count_z)
    extended = jnp.concatenate([blocks, jnp.roll(blocks[:, :1], -1, axis=0)], axis=1)
    product = jnp.einsum("ij,pjyz->piyz", stiffness, extended, precision=lax.Precision.HIGHEST)
    folded = jnp.concatenate([product[:, :1] + jnp.roll(product[:, 7:8], 1, axis=0), product[:, 1:7]], axis=1)
    return folded.reshape(planes, count_y, count_z)


def combine(grid_values, screening, stiff_x_part, mass_x, tables_list):
    stiffness, mass_edge, stiff_y = tables_list[0], tables_list[1], tables_list[4]
    mass_z = jnp.repeat(mass_edge, grid_values.shape[2] // 7)[None, None, :]
    mass_yy = tables_list[3][None, :, None]
    mass_xx = mass_x[:, None, None]
    return (mass_xx * mass_yy * mass_z * screening * grid_values + mass_yy * mass_z * stiff_x_part
            + mass_xx * mass_z * stiff_along_y(grid_values, stiff_y)
            + mass_xx * mass_yy * stiff_along_z(grid_values, stiffness))


def diagonal(screening, mass_x, stiff_x_diag, tables_list):
    elems_z = screening.shape[2] // 7
    mass_z = jnp.repeat(tables_list[1], elems_z)[None, None, :]
    stiff_z_diag = jnp.repeat(tables_list[2], elems_z)[None, None, :]
    mass_yy = tables_list[3][None, :, None]
    stiff_y_diag = tables_list[5][None, :, None]
    mass_xx = mass_x[:, None, None]
    return (mass_xx * mass_yy * mass_z * screening + mass_yy * mass_z * stiff_x_diag[:, None, None]
            + mass_xx * mass_z * stiff_y_diag + mass_xx * mass_yy * stiff_z_diag)


def restrict_yz(grid_values, tables_list):
    planes, count_y, count_z = grid_values.shape
    element_view = grid_values.reshape(planes, count_y, 7, count_z // 7)
    share_low = jnp.einsum("i,xyiz->xyz", tables_list[7], element_view, precision=lax.Precision.HIGHEST)
    share_high = jnp.einsum("i,xyiz->xyz", tables_list[8], element_view, precision=lax.Precision.HIGHEST)
    along_z = share_low + jnp.roll(share_high, 1, axis=2)
    return jnp.einsum("mv,xmz->xvz", tables_list[6], along_z, precision=lax.Precision.HIGHEST)


def prolong_yz(coarse_x, tables_list):
    fine_y = jnp.einsum("mv,xvz->xmz", tables_list[6], coarse_x, precision=lax.Precision.HIGHEST)
    phi_low = tables_list[7][None, None, :, None]
    phi_high = tables_list[8][None, None, :, None]
    fine_z = phi_low * fine_y[:, :, None, :] + phi_high * jnp.roll(fine_y, -1, axis=2)[:, :, None, :]
    planes, count_y, elems_z = fine_y.shape
    return fine_z.reshape(planes, count_y, 7 * elems_z)


def coarse_operator(values, lower_values, upper_values, coarse_screen, tables_list):
    mass_cy = tables_list[10][:, None]
    along_y = jnp.einsum("uv,...vz->...uz", tables_list[9], values, precision=lax.Precision.HIGHEST)
    along_z = values - 0.5 * (jnp.roll(values, 1, axis=-1) + jnp.roll(values, -1, axis=-1))
    along_x = values - 0.5 * (lower_values + upper_values)
    return 4.0 * mass_cy * coarse_screen * values + 2.0 * mass_cy * along_x + 4.0 * along_y + 2.0 * mass_cy * along_z


def coarse_diagonal(coarse_screen, tables_list):
    mass_cy = tables_list[10][:, None]
    return 4.0 * mass_cy * coarse_screen + 4.0 * mass_cy + 4.0 * tables_list[11][:, None]


def jacobi(coarse_rhs, coarse_screen, neighbours, tables_list):
    diag_c = coarse_diagonal(coarse_screen, tables_list)
    solution = damping * coarse_rhs / diag_c
    for sweep_index in range(CSWEEPS - 1):
        lower_values, upper_values = neighbours(solution)
        solution = solution + damping * (coarse_rhs - coarse_operator(solution, lower_values, upper_values, coarse_screen, tables_list)) / diag_c
    return solution


def roll_neighbours(values):
    return jnp.roll(values, 1, axis=0), jnp.roll(values, -1, axis=0)


def precondition(residual, screening, diag_a, tables_list):
    along_y = restrict_yz(residual, tables_list)
    planes = along_y.shape[0]
    element_view = along_y.reshape(planes // 7, 7, along_y.shape[1], along_y.shape[2])
    share_low = jnp.einsum("i,pivz->pvz", tables_list[7], element_view, precision=lax.Precision.HIGHEST)
    share_high = jnp.einsum("i,pivz->pvz", tables_list[8], element_view, precision=lax.Precision.HIGHEST)
    coarse_rhs = share_low + jnp.roll(share_high, 1, axis=0)
    coarse_screen = screening[::7, ::7, :EZ]
    solution = jacobi(coarse_rhs, coarse_screen, roll_neighbours, tables_list)
    upper_values = jnp.roll(solution, -1, axis=0)
    fine_x = tables_list[7][None, :, None, None] * solution[:, None] + tables_list[8][None, :, None, None] * upper_values[:, None]
    fine_x = fine_x.reshape(planes, along_y.shape[1], along_y.shape[2])
    return residual / diag_a + prolong_yz(fine_x, tables_list)


def reference(right_side, screening):
    tables_list = tables(EY)
    count_x = right_side.shape[0]
    mass_x = jnp.tile(tables_list[1], count_x // 7)
    stiff_x_diag = jnp.tile(tables_list[2], count_x // 7)
    diag_a = diagonal(screening, mass_x, stiff_x_diag, tables_list)

    def apply_operator(grid_values):
        return combine(grid_values, screening, stiff_along_x(grid_values, tables_list[0]), mass_x, tables_list)

    solution_field = jnp.zeros_like(right_side)
    residual = right_side
    precond = precondition(residual, screening, diag_a, tables_list)
    direction = precond
    rho_now = jnp.sum(residual * precond)
    for iteration in range(ITERS):
        operated = apply_operator(direction)
        step_length = rho_now / jnp.sum(direction * operated)
        solution_field = solution_field + step_length * direction
        residual = residual - step_length * operated
        if iteration + 1 < ITERS:
            precond = precondition(residual, screening, diag_a, tables_list)
            rho_next = jnp.sum(residual * precond)
            direction = precond + (rho_next / rho_now) * direction
            rho_now = rho_next
    return solution_field, residual
```

```python
import functools

import jax
import jax.numpy as jnp
import numpy as np
from jax import lax
from jax.experimental import pallas as pl
from jax.experimental.pallas import tpu as pltpu
from jax.sharding import Mesh
from jax.sharding import PartitionSpec as P

def legendre_seven(points):
    return (429.0 * points**7 - 693.0 * points**5 + 315.0 * points**3 - 35.0 * points) / 16.0


def pad_vector(vector, before, after):
    return np.concatenate([np.zeros(before), vector, np.zeros(after)])


def pad_matrix(matrix, before, after):
    width = matrix.shape[1]
    rows = np.concatenate([np.zeros((before, width)), matrix, np.zeros((after, width))], axis=0)
    height = rows.shape[0]
    return np.concatenate([np.zeros((height, before)), rows, np.zeros((height, after))], axis=1)


def diag_entries(matrix):
    return np.array([matrix[k, k] for k in range(matrix.shape[0])])


def diag_matrix(vector):
    count = vector.shape[0]
    return np.stack([pad_vector(np.array([vector[k]]), k, count - 1 - k) for k in range(count)])


def gll_tables():
    gll_nodes = np.array(
        [
            -1.0,
            -0.8717401485096066,
            -0.5917001814331423,
            -0.2092992179024789,
            0.2092992179024789,
            0.5917001814331423,
            0.8717401485096066,
            1.0,
        ]
    )
    values = legendre_seven(gll_nodes)
    weights = 2.0 / (56.0 * values * values)
    spacing = gll_nodes[:, None] - gll_nodes[None, :]
    distinct = np.abs(spacing) > 1e-12
    divisor = np.where(distinct, spacing, 1.0)
    derivative = np.where(distinct, values[:, None] / values[None, :] / divisor, 0.0)
    derivative = derivative + diag_matrix(np.array([-14.0, 0.0, 0.0, 0.0, 0.0, 0.0, 0.0, 14.0]))
    stiffness = derivative.T @ (weights[:, None] * derivative)
    return (gll_nodes, weights, stiffness)


CSWEEPS = 3
damping = 0.6
EY = 3
NY = 7 * EY + 1
PY = 24
LANES = 128
ROWS = 7 * PY
FULL = 8 * PY
AXES = ("x", "y", "z", "core")
GRID = {512: (4, 4, 16, 2)}
VMEM_BYTES = 24 * 1024 * 1024


class Tables:
    def __init__(self):
        nodes, w, K = gll_tables()
        self.K = K
        low = (1.0 - nodes) / 2.0
        high = (1.0 + nodes) / 2.0
        self.low, self.high = low, high
        mass = np.concatenate([[w[0] + w[7]], w[1:7]])
        kdiag = np.diag(K)
        stiff = np.concatenate([[kdiag[0] + kdiag[7]], kdiag[1:7]])
        self.mass, self.stiff = mass, stiff
        my = np.zeros(PY)
        Ky = np.zeros((PY, PY))
        interp = np.zeros((PY, EY + 1))
        q = np.zeros((EY + 1, EY + 1))
        for e in range(EY):
            my[7 * e : 7 * e + 8] += w
            Ky[7 * e : 7 * e + 8, 7 * e : 7 * e + 8] += K
            q[e : e + 2, e : e + 2] += np.array([[0.5, -0.5], [-0.5, 0.5]])
        for n in range(NY):
            e = min(n // 7, EY - 1)
            interp[n, e] = low[n - 7 * e]
            interp[n, e + 1] = high[n - 7 * e]
        self.my, self.interp = my, interp
        real = (np.arange(PY) < NY).astype(np.float64)
        cy = np.array([1.0] + [2.0] * (EY - 1) + [1.0])
        wxy = np.zeros((FULL, FULL))
        for i in range(8):
            for j in range(8):
                block = K[i, j] * np.diag(my)
                if i == j and i < 7:
                    block = block + mass[i] * Ky
                wxy[PY * i : PY * i + PY, PY * j : PY * j + PY] = block
        self.wxy = wxy[:ROWS]
        p1 = np.concatenate([my * stiff[i] + mass[i] * np.diag(Ky) + (1.0 - real) for i in range(7)])
        p2 = np.concatenate([my * mass[i] for i in range(7)])
        rest = np.zeros((8, ROWS))
        for i in range(7):
            rest[0:4, PY * i : PY * i + PY] = low[i] * interp.T
            rest[4:8, PY * i : PY * i + PY] = high[i] * interp.T
        self.rest = rest
        alpha = float(np.dot(K[7, :7], low[:7]))
        beta = float(np.dot(K[7, :7], high[:7]))
        prol = np.zeros((FULL + PY, 16))
        for i in range(8):
            prol[PY * i : PY * i + PY, 4:8] = low[i] * interp
            prol[PY * i : PY * i + PY, 8:12] = high[i] * interp
        prol[FULL:, 0:4] = my[:, None] * (alpha * interp)
        prol[FULL:, 4:8] = my[:, None] * (beta * interp)
        self.prol = prol
        wide = lambda v: np.repeat(np.asarray(v)[:, None], LANES, axis=1)
        self.col = np.concatenate([wide(p1), wide(p2), wide(my)], axis=0).astype(np.float32)
        self.coarse = np.concatenate([wide(cy), wide(4.0 * cy + 4.0 * np.diag(q))], axis=0).astype(np.float32)


def split(matrix):
    matrix = np.asarray(matrix, np.float32)
    top = matrix.astype(jnp.bfloat16)
    return np.stack([top, (matrix - top.astype(np.float32)).astype(jnp.bfloat16)])


def dot(a, b):
    return jnp.dot(a, b, preferred_element_type=jnp.float32)


def split_dot(m_ref, value):
    top = value.astype(jnp.bfloat16)
    rest = (value - top.astype(jnp.float32)).astype(jnp.bfloat16)
    return dot(m_ref[0], top) + (dot(m_ref[0], rest) + dot(m_ref[1], top))


def up_one(value):
    return pltpu.roll(value, LANES - 1, 1)


def down_one(value):
    return pltpu.roll(value, 1, 1)


def tile(j):
    return slice(LANES * j, LANES * j + LANES)


def plane_rows(i):
    return slice(PY * i, PY * i + PY)


def head(t, field, dinv_ref, screen4, first, rest_ref, my_rows, u_ref, msib_ref, xout_ref):
    seven = [None] * 7
    for j in range(7):
        for i in range(7):
            u = field[plane_rows(i), tile(j)] * dinv_ref[plane_rows(i), tile(j)]
            u_ref[plane_rows(i), tile(j)] = u
            term = float(t.K[7, i]) * u
            seven[j] = term if i == 0 else seven[j] + term
    for j in range(7):
        seven_plane = (my_rows * seven[j]) * float(t.mass[j])
        zero_plane = u_ref[0:PY, tile(j)]
        xout_ref[PY * j : PY * j + PY, :] = jnp.where(first, zero_plane, seven_plane)
        msib_ref[PY * j : PY * j + PY, :] = jnp.where(first, seven_plane, zero_plane)
    low = float(t.low[0]) * field[:, tile(0)]
    high = float(t.high[1]) * field[:, tile(1)]
    for i in range(1, 7):
        low = low + float(t.low[i]) * field[:, tile(i)]
    for i in range(2, 7):
        high = high + float(t.high[i]) * field[:, tile(i)]
    along_z = low + down_one(high)
    msib_ref[ROWS : ROWS + 8, :] = split_dot(rest_ref, along_z)
    msib_ref[ROWS + 8 : ROWS + 12, :] = screen4
    msib_ref[ROWS + 12 : ROWS + 16, :] = jnp.zeros_like(screen4)


def first_kernel(t, r_ref, s_ref, col_ref, rest_ref, rp_ref, u_ref, dinv_ref, sm_ref, msib_ref, xout_ref):
    first = lax.axis_index("core") == 0
    zero = jnp.zeros((8, 7 * LANES), jnp.float32)
    for i in range(7):
        rp_ref[PY * i + 16 : PY * i + PY, :] = zero
        sm_ref[PY * i + 16 : PY * i + PY, :] = zero
        rp_ref[PY * i : PY * i + NY, :] = r_ref[i]
        sm_ref[PY * i : PY * i + NY, :] = s_ref[i]
    screen4 = jnp.concatenate([sm_ref[7 * q : 7 * q + 1, 0:LANES] for q in range(EY + 1)], axis=0)
    my_rows = col_ref[2 * ROWS : 2 * ROWS + PY, :]
    for i in range(7):
        p1 = col_ref[PY * i : PY * i + PY, :]
        p2 = col_ref[ROWS + PY * i : ROWS + PY * i + PY, :]
        for j in range(7):
            sm = (p2 * float(t.mass[j])) * sm_ref[plane_rows(i), tile(j)]
            sm_ref[plane_rows(i), tile(j)] = sm
            diag = sm + float(t.mass[j]) * p1 + float(t.stiff[j]) * p2
            dinv_ref[plane_rows(i), tile(j)] = 1.0 / diag
    head(t, rp_ref, dinv_ref, screen4, first, rest_ref, my_rows, u_ref, msib_ref, xout_ref)


def coarse_solve(packs, coarse_ref, second):
    cy = coarse_ref[0:4, :]
    base = coarse_ref[4:8, :]
    zero_row = jnp.zeros((1, LANES), jnp.float32)
    rhs, gain, values = {}, {}, {}
    for v in range(1, 9):
        rhs[v] = packs[v][0:4] + packs[v - 1][4:8]
        gain[v] = damping / (4.0 * cy * packs[v][8:12] + base)
        values[v] = gain[v] * rhs[v]
    for sweep in range(1, CSWEEPS):
        new = {}
        for v in range(1 + sweep, 9 - sweep):
            c = values[v]
            sides = values[v - 1] + values[v + 1] + up_one(c) + down_one(c)
            walls = jnp.concatenate([zero_row, c[0:3]], axis=0) + jnp.concatenate([c[1:4], zero_row], axis=0)
            new[v] = (1.0 - damping) * c + gain[v] * (rhs[v] + cy * sides + 2.0 * walls)
        values = new
    picked = [jnp.where(second, values[v + 1], values[v]) for v in (3, 4, 5)]
    return jnp.concatenate(picked + [jnp.zeros((4, LANES), jnp.float32)], axis=0)


def tail(t, u_ref, sm_ref, col_ref, ag1_ref, recv_ref, ag2_ref, coarse_ref, prol_ref, wxy_ref, z_ref, w_ref, full_ref, second):
    packs = []
    order = [(2, 0, 32), (2, 0, 48), (2, 0, 0), (2, 0, 16), (1, 0, ROWS), (1, 1, ROWS), (2, 1, 0), (2, 1, 16), (2, 1, 32), (2, 1, 48)]
    for which, core, row in order:
        ref = ag1_ref if which == 1 else ag2_ref
        packs.append(ref[core, row : row + 12, :])
    c = coarse_solve(packs, coarse_ref, second)
    fine = split_dot(prol_ref, c)
    fine_up = up_one(fine)
    my_rows = col_ref[2 * ROWS : 2 * ROWS + PY, :]
    incoming = []
    for j in range(7):
        f = float(t.low[j]) * fine + float(t.high[j]) * fine_up if j else fine
        sib0, sib1 = ag1_ref[0, PY * j : PY * j + PY, :], ag1_ref[1, PY * j : PY * j + PY, :]
        outer = recv_ref[PY * j : PY * j + PY, :]
        zero_plane = jnp.where(second, outer, sib1)
        seven_plane = jnp.where(second, sib0, outer)
        full_ref[0:ROWS, tile(j)] = u_ref[:, tile(j)] + f[0:ROWS]
        full_ref[ROWS:FULL, tile(j)] = zero_plane + f[ROWS:FULL]
        own = u_ref[0:PY, tile(j)]
        incoming.append(seven_plane + float(t.mass[j]) * (f[FULL : FULL + PY] + float(t.K[7, 7]) * my_rows * (own + f[0:PY])))
    xy = split_dot(wxy_ref, full_ref[...])
    K = t.K
    for i in range(7):
        p2 = col_ref[ROWS + PY * i : ROWS + PY * i + PY, :]
        parts = [full_ref[plane_rows(i), tile(j)] for j in range(7)]
        parts.append(up_one(parts[0]))
        out = []
        for m in range(8):
            acc = float(K[m, 0]) * parts[0]
            for j in range(1, 8):
                acc = acc + float(K[m, j]) * parts[j]
            out.append(acc)
        out[0] = out[0] + down_one(out[7])
        for j in range(7):
            w = sm_ref[plane_rows(i), tile(j)] * parts[j] + p2 * out[j] + float(t.mass[j]) * xy[plane_rows(i), tile(j)]
            if i == 0:
                w = w + incoming[j]
            w_ref[plane_rows(i), tile(j)] = w
            z_ref[plane_rows(i), tile(j)] = parts[j]


def partial(a_ref, b_ref):
    total = None
    for i in range(7):
        for j in range(7):
            term = a_ref[plane_rows(i), tile(j)] * b_ref[plane_rows(i), tile(j)]
            total = term if total is None else total + term
    return total[0:8] + total[8:16] + total[16:24]


def second_kernel(t, rp_ref, u_ref, dinv_ref, sm_ref, col_ref, rest_ref, coarse_ref, prol_ref, wxy_ref, ag1_ref, recv_ref, ag2_ref,
                  z_ref, w_ref, u2_ref, msib_ref, xout_ref, sums_ref, full_ref):
    core = lax.axis_index("core")
    tail(t, u_ref, sm_ref, col_ref, ag1_ref, recv_ref, ag2_ref, coarse_ref, prol_ref, wxy_ref, z_ref, w_ref, full_ref, core == 1)
    screen4 = jnp.where(core == 1, ag1_ref[1, ROWS + 8 : ROWS + 12, :], ag1_ref[0, ROWS + 8 : ROWS + 12, :])
    my_rows = col_ref[2 * ROWS : 2 * ROWS + PY, :]
    head(t, w_ref, dinv_ref, screen4, core == 0, rest_ref, my_rows, u2_ref, msib_ref, xout_ref)
    sums_ref[0:8, :] = partial(rp_ref, z_ref)
    sums_ref[8:16, :] = partial(z_ref, w_ref)


def third_kernel(t, w_ref, u_ref, sm_ref, col_ref, coarse_ref, prol_ref, wxy_ref, ag1_ref, recv_ref, ag2_ref, sums_in_ref,
                 v_ref, y_ref, sums_ref, full_ref):
    core = lax.axis_index("core")
    tail(t, u_ref, sm_ref, col_ref, ag1_ref, recv_ref, ag2_ref, coarse_ref, prol_ref, wxy_ref, v_ref, y_ref, full_ref, core == 1)
    groups = [sums_in_ref[0:8, :], sums_in_ref[8:16, :], partial(w_ref, v_ref), partial(v_ref, y_ref)]
    lane = lax.broadcasted_iota(jnp.int32, (1, LANES), 1) // 32
    row = jnp.zeros((1, LANES), jnp.float32)
    for k in range(4):
        total = jnp.sum(groups[k], axis=0, keepdims=True)
        total = total + pltpu.roll(total, 64, 1)
        total = total + pltpu.roll(total, 32, 1)
        row = jnp.where(lane == k, total, row)
    for g in range(sums_ref.shape[0]):
        sums_ref[g] = row


def spread_kernel(got_ref, out_ref):
    total = got_ref[0]
    for g in range(1, got_ref.shape[0]):
        total = total + got_ref[g]
    for g in range(out_ref.shape[0]):
        out_ref[g] = total


def last_kernel(r_ref, z_ref, w_ref, v_ref, y_ref, got_ref, x_ref, res_ref):
    total = got_ref[0]
    for g in range(1, got_ref.shape[0]):
        total = total + got_ref[g]
    lane = lax.broadcasted_iota(jnp.int32, (1, LANES), 1) // 32
    rho, pi, sigma, tau = [jnp.sum(jnp.where(lane == k, total, 0.0), axis=1, keepdims=True) for k in range(4)]
    step0 = rho / pi
    rho1 = step0 * step0 * sigma - rho
    ratio = 1.0 + rho1 / rho
    step1 = rho1 / (ratio * ratio * pi - 2.0 * ratio * step0 * sigma + step0 * step0 * tau)
    a = step0 + step1 * ratio
    b = step1 * step0
    for i in range(7):
        rows = slice(PY * i, PY * i + NY)
        x_ref[i] = a * z_ref[rows, :] - b * v_ref[rows, :]
        res_ref[i] = r_ref[i] - a * w_ref[rows, :] + b * y_ref[rows, :]


def f32(*shape):
    return jax.ShapeDtypeStruct(shape, jnp.float32)


def call(kernel, outs, args, scratch=(), name=None):
    space = pl.BlockSpec(memory_space=pltpu.VMEM)
    return pl.pallas_call(
        kernel,
        out_shape=outs,
        in_specs=[space] * len(args),
        out_specs=[space] * len(outs) if isinstance(outs, (list, tuple)) else space,
        scratch_shapes=list(scratch),
        compiler_params=pltpu.CompilerParams(vmem_limit_bytes=VMEM_BYTES),
        name=name,
    )(*args)


def chip_permute(block, distance):
    count = 1
    for axis in AXES:
        count *= lax.axis_size(axis)
    chips = count // 2
    route = []
    for device in range(count):
        chip, core = divmod(device, 2)
        route.append((device, 2 * ((chip + distance) % chips) if core else 2 * ((chip - distance) % chips) + 1))
    return lax.ppermute(block, AXES, route)


def halo(msib, xout):
    ag1 = lax.all_gather(msib, "core")
    packs = ag1[:, ROWS:, :].reshape(32, LANES)
    far = chip_permute(packs, 2)
    near = chip_permute(jnp.concatenate([xout, packs], axis=0), 1)
    ag2 = lax.all_gather(jnp.concatenate([near[ROWS:], far], axis=0), "core")
    return ag1, near, ag2


def per_device(right_side, screening):
    t = Tables()
    col = jnp.asarray(t.col)
    coarse = jnp.asarray(t.coarse)
    rest, prol, wxy = (jnp.asarray(split(m)) for m in (t.rest, t.prol, t.wxy))
    big = f32(ROWS, 7 * LANES)
    msg = [f32(ROWS + 16, LANES), f32(ROWS, LANES)]
    rp, u, dinv, sm, msib, xout = call(
        functools.partial(first_kernel, t), [big] * 4 + msg, (right_side, screening, col, rest), name="first"
    )
    ag1, near, ag2 = halo(msib, xout)
    full = pltpu.VMEM((FULL, 7 * LANES), jnp.float32)
    z, w, u2, msib, xout, sums = call(
        functools.partial(second_kernel, t), [big] * 3 + msg + [f32(16, LANES)],
        (rp, u, dinv, sm, col, rest, coarse, prol, wxy, ag1, near, ag2), [full], name="second",
    )
    ag1, near, ag2 = halo(msib, xout)
    groups = lax.axis_size(("x", "y"))
    rest_count = lax.axis_size(("z", "core"))
    v, y, sums = call(
        functools.partial(third_kernel, t), [big, big, f32(groups, 1, LANES)],
        (w, u2, sm, col, coarse, prol, wxy, ag1, near, ag2, sums), [full], name="third",
    )
    got = lax.all_to_all(sums, ("x", "y"), 0, 0, tiled=True)
    sums = call(spread_kernel, f32(rest_count, 1, LANES), (got,), name="spread")
    got = lax.all_to_all(sums, ("z", "core"), 0, 0, tiled=True)
    return call(last_kernel, [f32(*right_side.shape)] * 2, (right_side, z, w, v, y, got), name="last")


def solution(mesh):
    devices = np.asarray(mesh.devices)
    shape = GRID.get(devices.size) or (1, 1, devices.size // 2, 2)
    fine_mesh = Mesh(devices.reshape(shape), AXES)
    spec = P(AXES, None, None)
    return jax.shard_map(per_device, mesh=fine_mesh, in_specs=(spec, spec), out_specs=(spec, spec), check_vma=False)
```

```python
import functools

import jax
import jax.numpy as jnp
import numpy as np
from jax import lax
from jax.experimental import pallas as pl
from jax.experimental.pallas import tpu as pltpu
from jax.sharding import Mesh
from jax.sharding import PartitionSpec as P

def legendre_seven(points):
    return (429.0 * points**7 - 693.0 * points**5 + 315.0 * points**3 - 35.0 * points) / 16.0


def pad_vector(vector, before, after):
    return np.concatenate([np.zeros(before), vector, np.zeros(after)])


def pad_matrix(matrix, before, after):
    width = matrix.shape[1]
    rows = np.concatenate([np.zeros((before, width)), matrix, np.zeros((after, width))], axis=0)
    height = rows.shape[0]
    return np.concatenate([np.zeros((height, before)), rows, np.zeros((height, after))], axis=1)


def diag_entries(matrix):
    return np.array([matrix[k, k] for k in range(matrix.shape[0])])


def diag_matrix(vector):
    count = vector.shape[0]
    return np.stack([pad_vector(np.array([vector[k]]), k, count - 1 - k) for k in range(count)])


def gll_tables():
    gll_nodes = np.array(
        [
            -1.0,
            -0.8717401485096066,
            -0.5917001814331423,
            -0.2092992179024789,
            0.2092992179024789,
            0.5917001814331423,
            0.8717401485096066,
            1.0,
        ]
    )
    values = legendre_seven(gll_nodes)
    weights = 2.0 / (56.0 * values * values)
    spacing = gll_nodes[:, None] - gll_nodes[None, :]
    distinct = np.abs(spacing) > 1e-12
    divisor = np.where(distinct, spacing, 1.0)
    derivative = np.where(distinct, values[:, None] / values[None, :] / divisor, 0.0)
    derivative = derivative + diag_matrix(np.array([-14.0, 0.0, 0.0, 0.0, 0.0, 0.0, 0.0, 14.0]))
    stiffness = derivative.T @ (weights[:, None] * derivative)
    return (gll_nodes, weights, stiffness)


CSWEEPS = 3
damping = 0.6
EY = 3
NY = 7 * EY + 1
PY = 24
LANES = 128
ROWS = 7 * PY
AXES = ("x", "y", "z", "core")
GRID = {512: (4, 4, 16, 2)}
VMEM_BYTES = 24 * 1024 * 1024
WIDE_VMEM_BYTES = 54784 * 1024
SIDE_FLOPS = 500_000_000


class Tables:
    def __init__(self):
        nodes, w, K = gll_tables()
        self.K = K
        low = (1.0 - nodes) / 2.0
        high = (1.0 + nodes) / 2.0
        self.low, self.high = low, high
        mass = np.concatenate([[w[0] + w[7]], w[1:7]])
        kdiag = np.diag(K)
        stiff = np.concatenate([[kdiag[0] + kdiag[7]], kdiag[1:7]])
        self.mass, self.stiff = mass, stiff
        my = np.zeros(PY)
        Ky = np.zeros((PY, PY))
        interp = np.zeros((PY, EY + 1))
        q = np.zeros((EY + 1, EY + 1))
        for e in range(EY):
            my[7 * e : 7 * e + 8] += w
            Ky[7 * e : 7 * e + 8, 7 * e : 7 * e + 8] += K
            q[e : e + 2, e : e + 2] += np.array([[0.5, -0.5], [-0.5, 0.5]])
        for n in range(NY):
            e = min(n // 7, EY - 1)
            interp[n, e] = low[n - 7 * e]
            interp[n, e + 1] = high[n - 7 * e]
        self.my, self.interp = my, interp
        real = (np.arange(PY) < NY).astype(np.float64)
        cy = np.array([1.0] + [2.0] * (EY - 1) + [1.0])
        wxy = np.zeros((ROWS, ROWS))
        for i in range(7):
            for j in range(7):
                block = K[i, j] * np.diag(my)
                if i == j:
                    block = block + mass[i] * Ky
                    if i == 0:
                        block = block + K[7, 7] * np.diag(my)
                wxy[PY * i : PY * i + PY, PY * j : PY * j + PY] = block
        self.wxy = wxy
        prol = np.zeros((2 * ROWS, 16))
        for i in range(7):
            prol[PY * i : PY * i + PY, 4:8] = low[i] * interp
            prol[PY * i : PY * i + PY, 8:12] = high[i] * interp
            rows = slice(ROWS + PY * i, ROWS + PY * i + PY)
            prol[rows, 4:8] = mass[i] * low[i] * (Ky @ interp)
            prol[rows, 8:12] = mass[i] * high[i] * (Ky @ interp)
        rows = slice(ROWS, ROWS + PY)
        prol[rows, 0:4] -= 0.5 * my[:, None] * interp
        prol[rows, 4:8] += my[:, None] * interp
        prol[rows, 8:12] -= 0.5 * my[:, None] * interp
        self.prol = prol
        wide = lambda v: np.repeat(np.asarray(v)[:, None], LANES, axis=1)
        self.rows = [my, np.diag(Ky), 1.0 - real] + [interp[:, k] for k in range(EY + 1)]
        tables = [wide(v) for v in self.rows] + [wide(cy), wide(4.0 * cy + 4.0 * np.diag(q))]
        self.col = np.concatenate(tables, axis=0).astype(np.float32)


def split(matrix):
    matrix = np.asarray(matrix, np.float32)
    top = matrix.astype(jnp.bfloat16)
    return np.stack([top, (matrix - top.astype(np.float32)).astype(jnp.bfloat16)])


def dot(a, b):
    return jnp.dot(a, b, preferred_element_type=jnp.float32)


def split_dot(m_ref, value):
    top = value.astype(jnp.bfloat16)
    rest = (value - top.astype(jnp.float32)).astype(jnp.bfloat16)
    return dot(m_ref[0], top) + (dot(m_ref[0], rest) + dot(m_ref[1], top))


def up_one(value):
    return pltpu.roll(value, LANES - 1, 1)


def down_one(value):
    return pltpu.roll(value, 1, 1)


def tile(j):
    return slice(LANES * j, LANES * j + LANES)


def plane_rows(i):
    return slice(PY * i, PY * i + PY)


def row_table(values):
    row = lax.broadcasted_iota(jnp.int32, (PY, LANES), 0)
    out = jnp.zeros((PY, LANES), jnp.float32)
    for n, value in enumerate(values):
        if value:
            out = jnp.where(row == n, float(value), out)
    return out


def row_tables(col_ref):
    return [col_ref[PY * k : PY * k + PY, :] for k in range(EY + 4)]


def head(t, field, dinv_ref, screen4, first, rows, u_ref, msib_ref, xout_ref):
    seven = [None] * 7
    for j in range(7):
        for i in range(7):
            u = field[plane_rows(i), tile(j)] * dinv_ref[plane_rows(i), tile(j)]
            u_ref[plane_rows(i), tile(j)] = u
            term = float(t.K[7, i]) * u
            seven[j] = term if i == 0 else seven[j] + term
    for j in range(7):
        seven_plane = (rows[0] * seven[j]) * float(t.mass[j])
        zero_plane = u_ref[0:PY, tile(j)]
        xout_ref[PY * j : PY * j + PY, :] = jnp.where(first, zero_plane, seven_plane)
        msib_ref[PY * j : PY * j + PY, :] = jnp.where(first, seven_plane, zero_plane)
    low = float(t.low[0]) * field[:, tile(0)]
    high = float(t.high[1]) * field[:, tile(1)]
    for i in range(1, 7):
        low = low + float(t.low[i]) * field[:, tile(i)]
    for i in range(2, 7):
        high = high + float(t.high[i]) * field[:, tile(i)]
    along_z = low + down_one(high)
    shares = [None, None]
    for i in range(7):
        for k, weight in enumerate((float(t.low[i]), float(t.high[i]))):
            if weight:
                term = weight * along_z[plane_rows(i)]
                shares[k] = term if shares[k] is None else shares[k] + term
    for k in range(2):
        for q in range(EY + 1):
            msib_ref[ROWS + 4 * k + q : ROWS + 4 * k + q + 1, :] = jnp.sum(shares[k] * rows[3 + q], axis=0, keepdims=True)
    msib_ref[ROWS + 8 : ROWS + 12, :] = screen4
    msib_ref[ROWS + 12 : ROWS + 16, :] = jnp.zeros_like(screen4)


def diagonal(t, s_ref, rows, dinv_ref, sm_ref):
    my_rows, ky_rows, pad_rows = rows[:3]
    zero = jnp.zeros((8, 7 * LANES), jnp.float32)
    for i in range(7):
        sm_ref[PY * i + 16 : PY * i + PY, :] = zero
        sm_ref[PY * i : PY * i + NY, :] = s_ref[i]
    screen4 = jnp.concatenate([sm_ref[7 * q : 7 * q + 1, 0:LANES] for q in range(EY + 1)], axis=0)
    for i in range(7):
        p1 = float(t.stiff[i]) * my_rows + float(t.mass[i]) * ky_rows + pad_rows
        p2 = float(t.mass[i]) * my_rows
        for j in range(7):
            sm = (p2 * float(t.mass[j])) * sm_ref[plane_rows(i), tile(j)]
            sm_ref[plane_rows(i), tile(j)] = sm
            diag = sm + float(t.mass[j]) * p1 + float(t.stiff[j]) * p2
            dinv_ref[plane_rows(i), tile(j)] = 1.0 / diag
    return screen4


def pad_planes(r_ref, rp_ref):
    zero = jnp.zeros((8, 7 * LANES), jnp.float32)
    for i in range(7):
        rp_ref[PY * i + 16 : PY * i + PY, :] = zero
        rp_ref[PY * i : PY * i + NY, :] = r_ref[i]


def first_kernel(t, r_hbm, s_hbm, msib_ref, xout_ref, r_ref, s_ref, rp_ref, u_ref, dinv_ref, sm_ref, sems):
    copies = [pltpu.make_async_copy(s_hbm, s_ref, sems.at[0]), pltpu.make_async_copy(r_hbm, r_ref, sems.at[1])]
    for copy in copies:
        copy.start()
    first = lax.axis_index("core") == 0
    rows = [row_table(v) for v in t.rows]
    copies[0].wait()
    screen4 = diagonal(t, s_ref, rows, dinv_ref, sm_ref)
    copies[1].wait()
    pad_planes(r_ref, rp_ref)
    head(t, rp_ref, dinv_ref, screen4, first, rows, u_ref, msib_ref, xout_ref)


def side_kernel(t, r_ref, s_ref, col_ref, wxy_ref, rp_ref, u_ref, dinv_ref, sm_ref, au_ref):
    diagonal(t, s_ref, row_tables(col_ref), dinv_ref, sm_ref)
    pad_planes(r_ref, rp_ref)
    for i in range(7):
        for j in range(7):
            u_ref[plane_rows(i), tile(j)] = rp_ref[plane_rows(i), tile(j)] * dinv_ref[plane_rows(i), tile(j)]
    apply_local(t, u_ref, sm_ref, col_ref, wxy_ref, au_ref)


def apply_local(t, u_ref, sm_ref, col_ref, wxy_ref, au_ref):
    xy = split_dot(wxy_ref, u_ref[...])
    my_rows = col_ref[0:PY, :]
    K = t.K
    for i in range(7):
        p2 = float(t.mass[i]) * my_rows
        parts = [u_ref[plane_rows(i), tile(j)] for j in range(7)]
        parts.append(up_one(parts[0]))
        out = []
        for m in range(8):
            acc = float(K[m, 0]) * parts[0]
            for j in range(1, 8):
                acc = acc + float(K[m, j]) * parts[j]
            out.append(acc)
        out[0] = out[0] + down_one(out[7])
        for j in range(7):
            au_ref[plane_rows(i), tile(j)] = (
                sm_ref[plane_rows(i), tile(j)] * parts[j] + p2 * out[j] + float(t.mass[j]) * xy[plane_rows(i), tile(j)]
            )


def partial(a_ref, b_ref):
    total = None
    for i in range(7):
        for j in range(7):
            term = a_ref[plane_rows(i), tile(j)] * b_ref[plane_rows(i), tile(j)]
            total = term if total is None else total + term
    return total[0:8] + total[8:16] + total[16:24]


def side_sums_kernel(t, u_ref, sm_ref, col_ref, wxy_ref, rp_ref, z_ref, w_ref, au_ref, sums_ref):
    apply_local(t, u_ref, sm_ref, col_ref, wxy_ref, au_ref)
    sums_ref[0:8, :] = partial(rp_ref, z_ref)
    sums_ref[8:16, :] = partial(z_ref, w_ref)


def coarse_solve(packs, coarse_ref, second):
    cy = coarse_ref[7 * PY : 7 * PY + 4, :]
    base = coarse_ref[7 * PY + 4 : 7 * PY + 8, :]
    zero_row = jnp.zeros((1, LANES), jnp.float32)
    rhs, gain, values = {}, {}, {}
    for v in range(1, 9):
        rhs[v] = packs[v][0:4] + packs[v - 1][4:8]
        gain[v] = damping / (4.0 * cy * packs[v][8:12] + base)
        values[v] = gain[v] * rhs[v]
    for sweep in range(1, CSWEEPS):
        new = {}
        for v in range(1 + sweep, 9 - sweep):
            c = values[v]
            sides = values[v - 1] + values[v + 1] + up_one(c) + down_one(c)
            walls = jnp.concatenate([zero_row, c[0:3]], axis=0) + jnp.concatenate([c[1:4], zero_row], axis=0)
            new[v] = (1.0 - damping) * c + gain[v] * (rhs[v] + cy * sides + 2.0 * walls)
        values = new
    picked = [jnp.where(second, values[v + 1], values[v]) for v in (3, 4, 5)]
    return jnp.concatenate(picked + [jnp.zeros((4, LANES), jnp.float32)], axis=0)


def tail(t, u_ref, au_ref, sm_ref, col_ref, prol_ref, ag1_ref, recv_ref, ag2_ref, z_ref, w_ref, second):
    order = [(2, 0, 32), (2, 0, 48), (2, 0, 0), (2, 0, 16), (1, 0, ROWS), (1, 1, ROWS), (2, 1, 0), (2, 1, 16), (2, 1, 32), (2, 1, 48)]
    packs = []
    for which, core, row in order:
        ref = ag1_ref if which == 1 else ag2_ref
        packs.append(ref[core, row : row + 12, :])
    c = coarse_solve(packs, col_ref, second)
    both = split_dot(prol_ref, c)
    my_rows = col_ref[0:PY, :]
    zero_planes, seven_planes = [], []
    for j in range(7):
        sib0, sib1 = ag1_ref[0, PY * j : PY * j + PY, :], ag1_ref[1, PY * j : PY * j + PY, :]
        outer = recv_ref[PY * j : PY * j + PY, :]
        zero_planes.append(my_rows * jnp.where(second, outer, sib1))
        seven_planes.append(jnp.where(second, sib0, outer))
    for i in range(7):
        f = both[plane_rows(i)]
        g = both[ROWS + PY * i : ROWS + PY * i + PY]
        f_up, g_up = up_one(f), up_one(g)
        bend = (float(t.mass[i]) * my_rows) * (f - 0.5 * (f_up + down_one(f)))
        for j in range(7):
            low, high, mass = float(t.low[j]), float(t.high[j]), float(t.mass[j])
            fine = low * f + high * f_up if j else f
            w = au_ref[plane_rows(i), tile(j)] + sm_ref[plane_rows(i), tile(j)] * fine
            w = w + ((mass * low) * g + (mass * high) * g_up if j else mass * g + bend)
            w = w + (mass * float(t.K[i, 7])) * zero_planes[j]
            if i == 0:
                w = w + seven_planes[j]
            w_ref[plane_rows(i), tile(j)] = w
            z_ref[plane_rows(i), tile(j)] = u_ref[plane_rows(i), tile(j)] + fine


def second_kernel(t, u_ref, au_ref, dinv_ref, sm_ref, col_ref, prol_ref, ag1_ref, recv_ref, ag2_ref,
                  z_ref, w_ref, u2_ref, msib_ref, xout_ref):
    core = lax.axis_index("core")
    tail(t, u_ref, au_ref, sm_ref, col_ref, prol_ref, ag1_ref, recv_ref, ag2_ref, z_ref, w_ref, core == 1)
    screen4 = jnp.where(core == 1, ag1_ref[1, ROWS + 8 : ROWS + 12, :], ag1_ref[0, ROWS + 8 : ROWS + 12, :])
    head(t, w_ref, dinv_ref, screen4, core == 0, row_tables(col_ref), u2_ref, msib_ref, xout_ref)


def third_kernel(t, w_ref, u_ref, au_ref, sm_ref, col_ref, prol_ref, ag1_ref, recv_ref, ag2_ref, sums_in_ref,
                 v_ref, y_ref, sums_ref):
    core = lax.axis_index("core")
    tail(t, u_ref, au_ref, sm_ref, col_ref, prol_ref, ag1_ref, recv_ref, ag2_ref, v_ref, y_ref, core == 1)
    groups = [sums_in_ref[0:8, :], sums_in_ref[8:16, :], partial(w_ref, v_ref), partial(v_ref, y_ref)]
    lane = lax.broadcasted_iota(jnp.int32, (1, LANES), 1) // 32
    row = jnp.zeros((1, LANES), jnp.float32)
    for k in range(4):
        total = jnp.sum(groups[k], axis=0, keepdims=True)
        total = total + pltpu.roll(total, 64, 1)
        total = total + pltpu.roll(total, 32, 1)
        row = jnp.where(lane == k, total, row)
    for g in range(sums_ref.shape[0]):
        sums_ref[g] = row


def spread_kernel(got_ref, out_ref):
    total = got_ref[0]
    for g in range(1, got_ref.shape[0]):
        total = total + got_ref[g]
    for g in range(out_ref.shape[0]):
        out_ref[g] = total


def last_kernel(rp_ref, z_ref, w_ref, v_ref, y_ref, got_ref, x_hbm, res_hbm, x_ref, res_ref, sems):
    total = got_ref[0]
    for g in range(1, got_ref.shape[0]):
        total = total + got_ref[g]
    lane = lax.broadcasted_iota(jnp.int32, (1, LANES), 1) // 32
    rho, pi, sigma, tau = [jnp.sum(jnp.where(lane == k, total, 0.0), axis=1, keepdims=True) for k in range(4)]
    step0 = rho / pi
    rho1 = step0 * step0 * sigma - rho
    ratio = 1.0 + rho1 / rho
    step1 = rho1 / (ratio * ratio * pi - 2.0 * ratio * step0 * sigma + step0 * step0 * tau)
    a = step0 + step1 * ratio
    b = step1 * step0
    copies = []
    for i in range(7):
        rows = slice(PY * i, PY * i + NY)
        x_ref[i] = a * z_ref[rows, :] - b * v_ref[rows, :]
        copies.append(pltpu.make_async_copy(x_ref.at[i], x_hbm.at[i], sems.at[0, i]))
        copies[-1].start()
        res_ref[i] = rp_ref[rows, :] - a * w_ref[rows, :] + b * y_ref[rows, :]
        copies.append(pltpu.make_async_copy(res_ref.at[i], res_hbm.at[i], sems.at[1, i]))
        copies[-1].start()
    for copy in copies:
        copy.wait()


def f32(*shape):
    return jax.ShapeDtypeStruct(shape, jnp.float32)


def call(kernel, outs, args, scratch=(), name=None, ins=pltpu.VMEM, out=pltpu.VMEM, flops=0, vmem=VMEM_BYTES):
    cost = pl.CostEstimate(flops=flops, bytes_accessed=flops // 64, transcendentals=0) if flops else None
    return pl.pallas_call(
        kernel,
        out_shape=outs,
        in_specs=[pl.BlockSpec(memory_space=ins)] * len(args),
        out_specs=[pl.BlockSpec(memory_space=out)] * len(outs) if isinstance(outs, (list, tuple)) else pl.BlockSpec(memory_space=out),
        scratch_shapes=list(scratch),
        compiler_params=pltpu.CompilerParams(vmem_limit_bytes=vmem),
        cost_estimate=cost,
        name=name,
    )(*args)


def chip_permute(block, distance):
    count = 1
    for axis in AXES:
        count *= lax.axis_size(axis)
    chips = count // 2
    route = []
    for device in range(count):
        chip, core = divmod(device, 2)
        route.append((device, 2 * ((chip + distance) % chips) if core else 2 * ((chip - distance) % chips) + 1))
    return lax.ppermute(block, AXES, route)


def halo(msib, xout):
    ag1 = lax.all_gather(msib, "core")
    packs = ag1[:, ROWS:, :].reshape(32, LANES)
    far = chip_permute(packs, 2)
    near = chip_permute(jnp.concatenate([xout, packs], axis=0), 1)
    ag2 = lax.all_gather(jnp.concatenate([near[ROWS:], far], axis=0), "core")
    return ag1, near, ag2


def per_device(right_side, screening):
    t = Tables()
    col = jnp.asarray(t.col)
    prol, wxy = (jnp.asarray(split(m)) for m in (t.prol, t.wxy))
    big = f32(ROWS, 7 * LANES)
    msg = [f32(ROWS + 16, LANES), f32(ROWS, LANES)]
    planes = pltpu.VMEM(right_side.shape, jnp.float32)
    padded = pltpu.VMEM(big.shape, jnp.float32)
    msib, xout = call(
        functools.partial(first_kernel, t), msg, (right_side, screening),
        [planes, planes] + [padded] * 4 + [pltpu.SemaphoreType.DMA((2,))], name="first", ins=pltpu.HBM, vmem=WIDE_VMEM_BYTES,
    )
    ag1, near, ag2 = halo(msib, xout)
    rp, u, dinv, sm, au = call(
        functools.partial(side_kernel, t), [big] * 5, (right_side, screening, col, wxy), name="side", flops=SIDE_FLOPS
    )
    z, w, u2, msib, xout = call(
        functools.partial(second_kernel, t), [big] * 3 + msg, (u, au, dinv, sm, col, prol, ag1, near, ag2), name="second"
    )
    ag1, near, ag2 = halo(msib, xout)
    au2, sums = call(
        functools.partial(side_sums_kernel, t), [big, f32(16, LANES)], (u2, sm, col, wxy, rp, z, w), name="side_sums", flops=SIDE_FLOPS
    )
    groups = lax.axis_size(("x", "y"))
    rest_count = lax.axis_size(("z", "core"))
    v, y, sums = call(
        functools.partial(third_kernel, t), [big, big, f32(groups, 1, LANES)],
        (w, u2, au2, sm, col, prol, ag1, near, ag2, sums), name="third",
    )
    got = lax.all_to_all(sums, ("x", "y"), 0, 0, tiled=True)
    sums = call(spread_kernel, f32(rest_count, 1, LANES), (got,), name="spread")
    got = lax.all_to_all(sums, ("z", "core"), 0, 0, tiled=True)
    return call(
        last_kernel, [f32(*right_side.shape)] * 2, (rp, z, w, v, y, got),
        [planes, planes, pltpu.SemaphoreType.DMA((2, 7))], name="last", out=pltpu.HBM,
    )


def solution(mesh):
    devices = np.asarray(mesh.devices)
    shape = GRID.get(devices.size) or (1, 1, devices.size // 2, 2)
    fine_mesh = Mesh(devices.reshape(shape), AXES)
    spec = P(AXES, None, None)
    return jax.shard_map(per_device, mesh=fine_mesh, in_specs=(spec, spec), out_specs=(spec, spec), check_vma=False)
```
